32 devices in a mesh: sub: 4 (over y, core), blk: 8 (over z, x).
Axes of the slice: x: 2, y: 2, z: 4, core: 2. Of those that a mesh axis runs over, the one named last changes fastest.
Arguments:
- face_loads: float32 [32, 5, 256, 128], P(('sub', 'blk')), may hold values from -6 to 6
- edge_mask: int32 [32, 5], P(('sub', 'blk')), may hold values from 0 to 1, as said below
- dof_map: int32 [32, 5, 256], P(('sub', 'blk')), may hold values from 0 to 255, as said below
- dual_op: float32 [32, 1280, 1280], P(('sub', 'blk')), as said below
- dirichlet: float32 [32, 1280, 1280], P(('sub', 'blk')), as said below
- coupling: float32 [32, 48, 1280], P(('sub', 'blk')), may hold values from -0.3125 to 0.3125
- corner_map: int32 [32, 48], replicated, may hold values from 0 to 1535, all different within a row
- coarse_inv: float32 [1536, 1536], P('blk'), as said below
Outputs:
- multipliers: float32 [32, 5, 256, 128], P(('sub', 'blk'))
- residual: float32 [32, 5, 256, 128], P(('sub', 'blk'))
The draws below stay inside these ranges and needn't reach their ends.
Inputs may be any that keep to these rules, and one draw needn't show every extreme that they name: edge_mask[s, r] equals edge_mask[partner(s, r), r]. Each dof_map[s, r] is a permutation of the 256 face unknowns, and dof_map[partner(s, r), r] is its inverse. Each dual_op[s] is symmetric positive definite. Each dirichlet[s] is symmetric positive definite. `coarse_inv`: symmetric positive definite. `corner_map`: a subdomain names 48 different coarse unknowns.
All inputs are finite; a program needn't handle non-finite values.
Results may differ from the reference program's by a relative error of at most 0.0003.
Values sent between devices are 32-bit elements; how exact they have to be, the bound alone decides.
A program may use at most 128 MiB of HBM per device.

```python
import math
import jax
import jax.numpy as jnp
from jax import lax

ROUNDS = 5
FACE_DOFS = 256
LOCAL_DOFS = 1280
LOADS = 128
CORNERS = 48
COARSE_DEV = 48
ITERS = 2
SUBDOMAINS = 32
COARSE = 1536
N_SUB = 4
N_BLK = 8


def edge_tables(key):
    count = N_SUB * N_BLK
    indices = jnp.arange(count, dtype=jnp.int32)
    offsets = jnp.array([2 ** colour if colour < 3 else N_BLK * 2 ** (colour - 3) for colour in range(ROUNDS)], dtype=jnp.int32)
    partner = jnp.bitwise_xor(indices[:, None], offsets[None, :])
    colours = jnp.arange(ROUNDS, dtype=jnp.int32)[None, :]
    keep = jax.random.randint(jax.random.fold_in(key, 11), (count, ROUNDS), 0, 4) < 3
    lower = jnp.minimum(indices[:, None], partner)
    mask = keep[lower, colours].astype(jnp.int32)
    keys = jax.random.split(jax.random.fold_in(key, 12), count * ROUNDS)
    base = jax.vmap(lambda single: jax.random.permutation(single, FACE_DOFS))(keys)
    base = base.reshape(count, ROUNDS, FACE_DOFS).astype(jnp.int32)
    inverse = jnp.argsort(base, axis=-1).astype(jnp.int32)
    is_lower = (indices[:, None] < partner)[:, :, None]
    perm = jnp.where(is_lower, base, inverse[partner, colours])
    return (mask, perm)


def draw_edge_mask(key, part):
    return edge_tables(key)[0]


def draw_dof_map(key, part):
    return edge_tables(key)[1]


def dominant(key, order, length, low, high):
    first, second, third = jax.random.split(key, 3)
    scales = jnp.exp(jax.random.uniform(first, (order,), jnp.float32, math.log(low), math.log(high)))
    places = jnp.arange(order, dtype=jnp.float32)
    kernel = jnp.exp(-jnp.abs(places[:, None] - places[None, :]) / length)
    rough = jax.random.uniform(second, (order, order), jnp.float32, -1.0, 1.0)
    rough = (rough + rough.T) * 0.5
    extra = jnp.exp(jax.random.uniform(third, (order,), jnp.float32, 0.0, math.log(4.0)))
    eye = jnp.eye(order, dtype=jnp.float32)
    smooth = scales[:, None] * scales[None, :] * kernel * (0.5 / length)
    return smooth + rough * (0.5 / order) + eye * (0.5 + 0.5 * extra)[:, None]


def draw_dual_op(key, part):
    key = jax.random.fold_in(key, 3)
    low, high = (0.5, 2.0)
    keys = jax.random.split(key, N_SUB * N_BLK)
    return lax.map(lambda single: dominant(single, ROUNDS * FACE_DOFS, 32.0, low, high), keys)


def draw_dirichlet(key, part):
    key = jax.random.fold_in(key, 4)
    low, high = (0.5, 2.0)
    keys = jax.random.split(key, N_SUB * N_BLK)
    return lax.map(lambda single: dominant(single, ROUNDS * FACE_DOFS, 24.0, low, high), keys)


def draw_coarse_inv(key, part):
    key = jax.random.fold_in(key, 5)
    low, high = (0.5, 2.0)
    return dominant(key, COARSE_DEV * N_SUB * N_BLK, 32.0, low, high)


def level_of(own_key, shape, cuts, low, top_value):
    factor_of = 1.0
    for axis_at, shards_of in cuts:
        heights = jax.random.uniform(jax.random.fold_in(jax.random.fold_in(own_key, 6), axis_at), (shards_of,), jnp.float32, low / len(cuts), top_value / len(cuts))
        factor_of = factor_of * jnp.repeat(jnp.exp(heights), shape[axis_at] // shards_of).reshape((-1,) + (1,) * (len(shape) - 1 - axis_at))
    return factor_of


def choose_distinct(rng, rows, number_of, top, lift):
    sequence = jax.random.permutation(jax.random.fold_in(rng, 1), number_of)
    boost = sequence
    for power in range(3):
        boost = boost * boost // number_of
    boost = boost * lift // number_of
    lots = jax.random.randint(jax.random.fold_in(rng, 2), (rows, number_of), 0, 4096) + boost
    fixed_rows = jax.random.permutation(jax.random.fold_in(rng, 3), rows)[jnp.arange(number_of) % rows]
    lots = jnp.where(jnp.arange(rows)[:, None] == fixed_rows[None, :], 1 << 14, lots)
    priority = lots * number_of + jnp.arange(number_of)
    return lax.top_k(priority.astype(jnp.int32), top)[1].astype(jnp.int32)


def noise(stream_key, extent, deviation, most, shards=(), held_as=jnp.bfloat16):
    drawn = jax.random.normal(stream_key, extent, jnp.float32) * deviation
    if len(shards) > 0:
        drawn = level_of(stream_key, extent, shards, -0.22, 0.18) * drawn
    return jnp.clip(drawn, min=-most, max=most).astype(held_as)


def setup_inputs(seed: int = 0) -> dict:
    seeds = jax.random.split(jax.random.key(seed), 9)
    face_loads = noise(seeds[0], (SUBDOMAINS, ROUNDS, FACE_DOFS, LOADS), 1.0, 6.0, ((0, 32),), jnp.float32)
    edge_mask = draw_edge_mask(jax.random.fold_in(seeds[8], 71), 0)
    dof_map = draw_dof_map(jax.random.fold_in(seeds[8], 71), 0)
    dual_op = draw_dual_op(jax.random.fold_in(seeds[8], 71), 0)
    dirichlet = draw_dirichlet(jax.random.fold_in(seeds[8], 71), 0)
    coupling = noise(seeds[5], (SUBDOMAINS, CORNERS, LOCAL_DOFS), (LOCAL_DOFS // 4) ** -0.5, 0.3125, ((0, 32),), jnp.float32)
    corner_map = choose_distinct(seeds[6], SUBDOMAINS, COARSE, CORNERS, 512)
    coarse_inv = draw_coarse_inv(jax.random.fold_in(seeds[8], 71), 0)
    return {"face_loads": face_loads, "edge_mask": edge_mask, "dof_map": dof_map, "dual_op": dual_op, "dirichlet": dirichlet, "coupling": coupling, "corner_map": corner_map, "coarse_inv": coarse_inv}


def partner_list():
    indices = jnp.arange(SUBDOMAINS, dtype=jnp.int32)
    offsets = [2 ** colour if colour < 3 else N_BLK * 2 ** (colour - 3) for colour in range(ROUNDS)]
    return [jnp.bitwise_xor(indices, jnp.int32(offset)) for offset in offsets]


def assemble(vector, edge_mask, dof_map):
    indices = jnp.arange(SUBDOMAINS, dtype=jnp.int32)
    pieces = []
    for colour, partner in enumerate(partner_list()):
        remote = vector[partner, colour]
        remote = remote[indices[:, None], dof_map[:, colour, :]]
        weight = edge_mask[:, colour].astype(jnp.float32)[:, None, None]
        pieces.append(weight * (vector[:, colour] - remote))
    return jnp.stack(pieces, axis=1)


def local_apply(matrix, vector):
    shaped = vector.reshape(SUBDOMAINS, LOCAL_DOFS, LOADS)
    result = jnp.einsum("sij,sjl->sil", matrix, shaped, precision=lax.Precision.HIGHEST)
    return result.reshape(vector.shape)


def coarse_term(vector, coupling, corner_map, coarse_inv):
    shaped = vector.reshape(SUBDOMAINS, LOCAL_DOFS, LOADS)
    partial_corner = jnp.einsum("scj,sjl->scl", coupling, shaped, precision=lax.Precision.HIGHEST)
    gathered = jax.ops.segment_sum(partial_corner.reshape(SUBDOMAINS * CORNERS, LOADS), corner_map.reshape(-1), num_segments=COARSE)
    solved = jnp.dot(coarse_inv, gathered, precision=lax.Precision.HIGHEST)
    corner_values = solved[corner_map]
    back = jnp.einsum("scj,scl->sjl", coupling, corner_values, precision=lax.Precision.HIGHEST)
    return back.reshape(vector.shape)


def reference(face_loads, edge_mask, dof_map, dual_op, dirichlet, coupling, corner_map, coarse_inv):
    def operator(vector):
        return assemble(local_apply(dual_op, vector) + coarse_term(vector, coupling, corner_map, coarse_inv), edge_mask, dof_map)

    def precondition(vector):
        return assemble(local_apply(dirichlet, vector), edge_mask, dof_map)

    residual = assemble(face_loads, edge_mask, dof_map)
    multipliers = jnp.zeros_like(residual)
    precond = precondition(residual)
    direction = precond
    inner_rz = jnp.sum(residual * precond, axis=(0, 1, 2))
    for sweep_idx in range(ITERS):
        image = operator(direction)
        alpha = inner_rz / jnp.sum(direction * image, axis=(0, 1, 2))
        multipliers = multipliers + alpha * direction
        residual = residual - alpha * image
        if sweep_idx + 1 < ITERS:
            precond = precondition(residual)
            rz_next = jnp.sum(residual * precond, axis=(0, 1, 2))
            direction = precond + (rz_next / inner_rz) * direction
            inner_rz = rz_next
    return multipliers, residual
```

```python
import functools

import jax
import jax.numpy as jnp
from jax import lax
from jax.experimental import pallas as pl
from jax.experimental.pallas import tpu as pltpu
from jax.sharding import PartitionSpec as P

ITERS = 2
COLOURS = 5
MESH = pl.DeviceIdType.MESH
ORDER = (2, 1, 0, 4, 3)
ARRIVAL = (3, 4, 0, 1, 2)
F32 = jnp.float32
BF16 = jnp.bfloat16


def split(value):
    high = value.astype(BF16)
    low = (value - high.astype(F32)).astype(BF16)
    return high, low


def both(value):
    high, low = split(value)
    return jnp.concatenate([high, low], axis=1)


def mul(left, right):
    return jnp.dot(left, right, preferred_element_type=F32)


def mul3(high, low, pair):
    lanes = pair.shape[1] // 2
    wide = mul(high, pair)
    return wide[:, :lanes] + wide[:, lanes:] + mul(low, pair[:, :lanes])


def fold(value):
    return jnp.sum(value.reshape(value.shape[0] // 8, 8, value.shape[1]), axis=0)


def kernel(
    n_sub, n_blk, group_rows, groups,
    face, mask, dof, dual, dirichlet, coupling, map_rows, map_cols, coarse,
    mult_out, res_out,
    stage, dir_hi, dir_lo, dual_hi, dual_lo, perm,
    coarse_stage, coarse_hi, coarse_lo, m_hi, m_lo, pick,
    cpl_hi, cpl_lo, cplt_hi, cplt_lo,
    vec, res, direc, image, y, step,
    j_send, j_recv, packed, x_recv, y_send, z_recv, d_send, d_recv,
    local_sem, j_ssem, j_rsem, x_ssem, x_rsem, z_ssem, z_rsem, d_ssem, d_rsem,
):
    n = n_sub * n_blk
    my_sub = lax.axis_index("sub")
    my_blk = lax.axis_index("blk")
    me = my_sub * n_blk + my_blk
    dofs = face.shape[2]
    lanes = face.shape[3]
    own = lanes // n_sub
    rows = pick.shape[0]
    width = coarse.shape[1]
    chunk = coarse_stage.shape[0]

    def device(t):
        return (t // n_blk, t % n_blk)

    load_dir = pltpu.make_async_copy(dirichlet.at[0], stage, local_sem.at[0])
    load_dir.start()
    load_coarse = [
        pltpu.make_async_copy(coarse.at[pl.ds(k * chunk, chunk)], coarse_stage, local_sem.at[1])
        for k in range(rows // chunk)
    ]
    load_coarse[0].start()

    barrier = pltpu.get_barrier_semaphore()

    def greet(k, carry):
        pl.semaphore_signal(barrier, inc=1, device_id=device((me + k) % n), device_id_type=MESH)
        return carry

    lax.fori_loop(1, n, greet, 0)

    for c in range(COLOURS):
        places = lax.broadcasted_iota(jnp.int32, (dofs, dofs), 0)
        perm[c] = jnp.where(places == dof[0, c : c + 1, :], 1.0, 0.0).astype(BF16)

    pl.semaphore_wait(barrier, n - 1)

    def partner(c):
        if c < 3:
            hop = 1 << c
            return (my_sub, my_blk + hop - 2 * hop * ((my_blk // hop) % 2))
        hop = 1 << (c - 3)
        return (my_sub + hop - 2 * hop * ((my_sub // hop) % 2), my_blk)

    def j_copy(j, c):
        return pltpu.make_async_remote_copy(
            src_ref=j_send.at[j, c],
            dst_ref=j_recv.at[j, c],
            send_sem=j_ssem.at[j, c],
            recv_sem=j_rsem.at[j, c],
            device_id=partner(c),
            device_id_type=MESH,
        )

    def j_start(j, c, value):
        wide = mul(perm[c], both(value))
        j_send[j, c] = wide[:, :lanes] + wide[:, lanes:]
        j_copy(j, c).start()

    def j_finish(j, c, value):
        j_copy(j, c).wait_recv()
        return mask[0, c].astype(F32) * (value - j_recv[j, c])

    def at(c):
        return pl.ds(c * dofs, dofs)

    def apply(high, low, c):
        return mul3(high[at(c), :], low[at(c), :], vec[...])

    def split_stage(high, low):
        def body(k, carry):
            part = pl.ds(pl.multiple_of(k * 128, 128), 128)
            h, l = split(stage[part, :])
            high[part, :] = h
            low[part, :] = l
            return carry

        lax.fori_loop(0, stage.shape[0] // 128, body, 0)

    def spread(make, count):
        def go(k, carry):
            make((me + k) % n).start()
            return carry

        lax.fori_loop(1, count, go, 0)

    def collect(make, count):
        def go(k, carry):
            make((me + k) % n).wait_recv()
            return carry

        lax.fori_loop(1, count, go, 0)

    def drain(make, count):
        def go(k, carry):
            make((me + k) % n).wait_send()
            return carry

        lax.fori_loop(1, count, go, 0)

    def to(src, dst, ssem, rsem):
        return lambda it, t, pos, landing: pltpu.make_async_remote_copy(
            src_ref=src(it, t), dst_ref=dst.at[it, landing], send_sem=ssem.at[it, t],
            recv_sem=rsem.at[it, pos], device_id=device(t), device_id_type=MESH,
        )

    x_any = to(lambda it, t: packed.at[it, t // n_blk], x_recv, x_ssem, x_rsem)
    z_any = to(lambda it, t: y_send.at[it, t], z_recv, z_ssem, z_rsem)
    d_any = to(lambda it, t: d_send.at[it], d_recv, d_ssem, d_rsem)

    def out(any_copy, it):
        return lambda t: any_copy(it, t, me, me)

    def back(any_copy, it):
        return lambda t: any_copy(it, t, t, t)

    lane = lax.broadcasted_iota(jnp.int32, (group_rows, lanes), 1) // own

    def coarse_send(it, rz_part):
        corner = mul3(cpl_hi[...], cpl_lo[...], vec[...])
        for a in range(n_sub):
            total = jnp.zeros((group_rows, lanes), F32)
            for g in range(groups):
                piece = corner[g * group_rows : (g + 1) * group_rows, :]
                turn = (own * (g - a)) % lanes
                moved = pltpu.roll(piece, turn, 1) if turn else piece
                total = jnp.where(lane == g, moved, total)
            packed[it, a, :group_rows, :] = total
            packed[it, a, group_rows:, :] = rz_part
        spread(out(x_any, it), n)
        x_recv[it, me] = packed[it, my_sub]

    def coarse_solve(it):
        collect(back(x_any, it), n)
        whole = x_recv[it]
        rz = jnp.sum(jnp.sum(whole[:, group_rows:, :], axis=0), axis=0, keepdims=True)
        x = whole[:, :group_rows, :].reshape(n * group_rows, lanes)
        mine = lax.broadcasted_iota(jnp.int32, (n * group_rows, lanes), 1) // own
        total = jnp.zeros((rows, lanes), F32)
        size = n * group_rows
        for g in range(groups):
            wide = mul(pick[:, g * size : (g + 1) * size], both(jnp.where(mine == g, x, 0.0)))
            total = total + wide[:, :lanes] + wide[:, lanes:]
        gathered = total
        for k in range(1, n_sub):
            gathered = gathered + pltpu.roll(total, own * k, 1)
        pair = both(gathered)
        result = jnp.zeros((size, lanes), F32)
        for g in range(groups):
            part = slice(g * size, (g + 1) * size)
            result = jnp.where(mine == g, mul3(m_hi[part, :], m_lo[part, :], pair), result)
        y_send[it] = result.reshape(n, group_rows, lanes)
        spread(out(z_any, it), n)
        z_recv[it, me] = y_send[it, me]
        return rz

    def coarse_back(it):
        collect(back(z_any, it), n)
        sums = [jnp.sum(z_recv[it, a * n_blk : (a + 1) * n_blk], axis=0) for a in range(n_sub)]
        pieces = []
        for g in range(groups):
            total = jnp.zeros((group_rows, lanes), F32)
            for a in range(n_sub):
                turn = (own * (a - g)) % lanes
                moved = pltpu.roll(sums[a], turn, 1) if turn else sums[a]
                total = jnp.where(lane == a, moved, total)
            pieces.append(total)
        return both(jnp.concatenate(pieces, axis=0))

    def dot_send(it, part):
        d_send[it] = part
        spread(out(d_any, it), n)
        d_recv[it, me] = part

    def dot_finish(it):
        collect(back(d_any, it), n)
        return jnp.sum(jnp.sum(d_recv[it], axis=0), axis=0, keepdims=True)

    for c in ORDER:
        j_start(0, c, face[0, c])
    load_dir.wait()
    split_stage(dir_hi, dir_lo)
    load_dual = pltpu.make_async_copy(dual.at[0], stage, local_sem.at[2])
    load_dual.start()
    cpl_hi[...], cpl_lo[...] = split(coupling[0])
    cplt_hi[...], cplt_lo[...] = split(coupling[0].T)
    for c in ARRIVAL:
        r = j_finish(0, c, face[0, c])
        res[c] = r
        vec[at(c), :] = both(r)

    for c in ORDER:
        y[c] = apply(dir_hi, dir_lo, c)
        j_start(1, c, y[c])
    load_dual.wait()
    split_stage(dual_hi, dual_lo)
    for g in range(groups):
        size = n * group_rows
        places = lax.broadcasted_iota(jnp.int32, (rows, size), 0) + my_blk * rows
        pick[:, g * size : (g + 1) * size] = jnp.where(
            places == map_rows[g : g + 1, :], 1.0, 0.0
        ).astype(BF16)
    rz_part = jnp.zeros((8, lanes), F32)
    for c in ARRIVAL:
        p = j_finish(1, c, y[c])
        direc[c] = p
        vec[at(c), :] = both(p)
        rz_part = rz_part + fold(res[c] * p)

    contract_last = (((1,), (1,)), ((), ()))
    alpha = None
    for it in range(ITERS):
        coarse_send(it, rz_part)
        for c in range(COLOURS):
            y[c] = apply(dual_hi, dual_lo, c)
        if it == 0:
            for k in range(rows // chunk):
                if k:
                    load_coarse[k].start()
                load_coarse[k].wait()
                coarse_hi[...], coarse_lo[...] = split(coarse_stage[...])

                def select(i, carry):
                    part = pl.ds(pl.multiple_of(i * 128, 128), 128)
                    places = lax.broadcasted_iota(jnp.int32, (128, width), 1)
                    chosen = jnp.where(places == map_cols[part, 0:1], 1.0, 0.0).astype(BF16)
                    for source, target in ((coarse_hi, m_hi), (coarse_lo, m_lo)):
                        target[part, k * chunk : (k + 1) * chunk] = lax.dot_general(
                            chosen, source[...], contract_last, preferred_element_type=F32
                        ).astype(BF16)
                    return carry

                lax.fori_loop(0, m_hi.shape[0] // 128, select, 0)
        rz_new = coarse_solve(it)
        corners = coarse_back(it)
        for c in ORDER:
            y[c] = y[c] + mul3(cplt_hi[at(c), :], cplt_lo[at(c), :], corners)
            j_start(2 + 2 * it, c, y[c])
        part = jnp.zeros((8, lanes), F32)
        if it == 0:
            rz = rz_new
            for c in ARRIVAL:
                i = j_finish(2, c, y[c])
                image[c] = i
                vec[at(c), :] = both(i)
                part = part + fold(direc[c] * i)
            dot_send(0, part)
            for c in ORDER:
                y[c] = apply(dir_hi, dir_lo, c)
                j_start(3, c, y[c])
            alpha = rz / dot_finish(0)
            rz_part = jnp.zeros((8, lanes), F32)
            for c in ARRIVAL:
                r = res[c] - alpha * image[c]
                res[c] = r
                p = direc[c] - alpha * j_finish(3, c, y[c])
                step[c] = p
                vec[at(c), :] = both(p)
                rz_part = rz_part + fold(r * p)
        else:
            beta = rz_new / rz
            for c in ARRIVAL:
                i = j_finish(4, c, y[c]) + beta * image[c]
                image[c] = i
                p = step[c] + beta * direc[c]
                step[c] = p
                part = part + fold(p * i)
            dot_send(1, part)
            last = rz_new / dot_finish(1)
            for c in range(COLOURS):
                mult_out[0, c] = alpha * direc[c] + last * step[c]
                res_out[0, c] = res[c] - last * image[c]

    for j in range(5):
        for c in range(COLOURS):
            j_copy(j, c).wait_send()
    for it in range(ITERS):
        for any_copy in (x_any, z_any, d_any):
            drain(out(any_copy, it), n)


def solution(mesh):
    n_sub, n_blk = mesh.shape["sub"], mesh.shape["blk"]
    n = n_sub * n_blk

    def shards(face, mask, dof, dual, dirichlet, coupling, corner_map, coarse):
        colours, dofs, lanes = face.shape[1:]
        local = colours * dofs
        corners = corner_map.shape[1]
        group_rows = -(-corners // (8 * n_sub)) * 8
        groups = corners // group_rows
        rows, width = coarse.shape
        chunk = rows if rows <= 192 else 128
        size = n * group_rows
        map_rows = (
            corner_map.reshape(n, groups, group_rows).transpose(1, 0, 2).reshape(groups, size)
        )
        map_cols = jnp.broadcast_to(map_rows.reshape(groups * size, 1), (groups * size, 128))
        vmem = pl.BlockSpec(memory_space=pltpu.VMEM)
        smem = pl.BlockSpec(memory_space=pltpu.SMEM)
        hbm = pl.BlockSpec(memory_space=pl.ANY)
        vector = pltpu.VMEM((colours, dofs, lanes), F32)
        dma = pltpu.SemaphoreType.DMA
        return pl.pallas_call(
            functools.partial(kernel, n_sub, n_blk, group_rows, groups),
            out_shape=[jax.ShapeDtypeStruct(face.shape, F32)] * 2,
            in_specs=[vmem, smem, vmem, hbm, hbm, vmem, vmem, vmem, hbm],
            out_specs=[vmem, vmem],
            scratch_shapes=[
                pltpu.VMEM((local, local), F32),
                pltpu.VMEM((local, local), BF16),
                pltpu.VMEM((local, local), BF16),
                pltpu.VMEM((local, local), BF16),
                pltpu.VMEM((local, local), BF16),
                pltpu.VMEM((colours, dofs, dofs), BF16),
                pltpu.VMEM((chunk, width), F32),
                pltpu.VMEM((chunk, width), BF16),
                pltpu.VMEM((chunk, width), BF16),
                pltpu.VMEM((groups * size, rows), BF16),
                pltpu.VMEM((groups * size, rows), BF16),
                pltpu.VMEM((rows, groups * size), BF16),
                pltpu.VMEM((corners, local), BF16),
                pltpu.VMEM((corners, local), BF16),
                pltpu.VMEM((local, corners), BF16),
                pltpu.VMEM((local, corners), BF16),
                pltpu.VMEM((local, 2 * lanes), BF16),
                vector, vector, vector, vector, vector,
                pltpu.VMEM((5, colours, dofs, lanes), F32),
                pltpu.VMEM((5, colours, dofs, lanes), F32),
                pltpu.VMEM((ITERS, n_sub, group_rows + 8, lanes), F32),
                pltpu.VMEM((ITERS, n, group_rows + 8, lanes), F32),
                pltpu.VMEM((ITERS, n, group_rows, lanes), F32),
                pltpu.VMEM((ITERS, n, group_rows, lanes), F32),
                pltpu.VMEM((ITERS, 8, lanes), F32),
                pltpu.VMEM((ITERS, n, 8, lanes), F32),
                dma((3,)),
                dma((5, colours)), dma((5, colours)),
                dma((ITERS, n)), dma((ITERS, n)),
                dma((ITERS, n)), dma((ITERS, n)),
                dma((ITERS, n)), dma((ITERS, n)),
            ],
            compiler_params=pltpu.CompilerParams(
                collective_id=0, has_side_effects=True, vmem_limit_bytes=62 << 20
            ),
            cost_estimate=pl.CostEstimate(
                flops=3 * 8 * local * local * lanes, bytes_accessed=8 * local * local,
                transcendentals=0,
            ),
        )(face, mask, dof, dual, dirichlet, coupling, map_rows, map_cols, coarse)

    split_first = P(("sub", "blk"), None, None, None)
    return jax.shard_map(
        shards,
        mesh=mesh,
        in_specs=(
            split_first,
            P(("sub", "blk"), None),
            P(("sub", "blk"), None, None),
            P(("sub", "blk"), None, None),
            P(("sub", "blk"), None, None),
            P(("sub", "blk"), None, None),
            P(),
            P("blk", None),
        ),
        out_specs=(split_first, split_first),
        check_vma=False,
    )
```

```python
import functools

import jax
import jax.numpy as jnp
from jax import lax
from jax.experimental import pallas as pl
from jax.experimental.pallas import tpu as pltpu
from jax.sharding import PartitionSpec as P

ITERS = 2
COLOURS = 5
MESH = pl.DeviceIdType.MESH
ORDER = (2, 1, 0, 4, 3)
ARRIVAL = (3, 4, 0, 1, 2)
F32 = jnp.float32
BF16 = jnp.bfloat16


def split(value):
    high = value.astype(BF16)
    low = (value - high.astype(F32)).astype(BF16)
    return high, low


def both(value):
    high, low = split(value)
    return jnp.concatenate([high, low], axis=1)


def mul(left, right):
    return jnp.dot(left, right, preferred_element_type=F32)


def mul3(high, low, pair):
    lanes = pair.shape[1] // 2
    wide = mul(high, pair)
    return wide[:, :lanes] + wide[:, lanes:] + mul(low, pair[:, :lanes])


def fold(value):
    return jnp.sum(value.reshape(value.shape[0] // 8, 8, value.shape[1]), axis=0)


def kernel(
    n_sub, n_blk, group_rows, groups,
    face, mask, dof, dual, dirichlet, coupling, map_rows, map_cols, coarse,
    direc, step, res, image, scales,
    stage, dir_hi, dir_lo, dual_hi, dual_lo, perm,
    coarse_stage, coarse_hi, coarse_lo, m_hi, m_lo, pick,
    cpl_hi, cpl_lo, cplt_hi, cplt_lo,
    vec, y, y_next,
    j_send, j_recv, packed, x_recv, y_send, z_recv, d_send, d_recv,
    local_sem, j_ssem, j_rsem, x_ssem, x_rsem, z_ssem, z_rsem, d_ssem, d_rsem,
):
    n = n_sub * n_blk
    my_sub = lax.axis_index("sub")
    my_blk = lax.axis_index("blk")
    me = my_sub * n_blk + my_blk
    dofs = face.shape[2]
    lanes = face.shape[3]
    own = lanes // n_sub
    rows = pick.shape[0]
    width = coarse.shape[1]
    chunk = coarse_stage.shape[0]

    def visit(act):
        for k in range(n_sub):
            sub_to = lax.rem(my_sub + k, n_sub)

            def go(j, carry):
                blk_to = lax.rem(my_blk + j, n_blk)
                act(sub_to, blk_to, sub_to * n_blk + blk_to)
                return carry

            lax.fori_loop(0 if k else 1, n_blk, go, 0)

    load_dir = pltpu.make_async_copy(dirichlet.at[0], stage, local_sem.at[0])
    load_dir.start()
    load_coarse = [
        pltpu.make_async_copy(coarse.at[pl.ds(k * chunk, chunk)], coarse_stage, local_sem.at[1])
        for k in range(rows // chunk)
    ]
    load_coarse[0].start()

    barrier = pltpu.get_barrier_semaphore()

    visit(
        lambda a, b, t: pl.semaphore_signal(
            barrier, inc=1, device_id=(a, b), device_id_type=MESH
        )
    )

    for c in range(COLOURS):
        places = lax.broadcasted_iota(jnp.int32, (dofs, dofs), 0)
        perm[c] = jnp.where(places == dof[c], 1.0, 0.0).astype(BF16)

    pl.semaphore_wait(barrier, n - 1)

    def partner(c):
        if c < 3:
            hop = 1 << c
            return (my_sub, my_blk + hop - 2 * hop * ((my_blk // hop) % 2))
        hop = 1 << (c - 3)
        return (my_sub + hop - 2 * hop * ((my_sub // hop) % 2), my_blk)

    def j_copy(j, c):
        return pltpu.make_async_remote_copy(
            src_ref=j_send.at[j, c],
            dst_ref=j_recv.at[j, c],
            send_sem=j_ssem.at[j, c],
            recv_sem=j_rsem.at[j, c],
            device_id=partner(c),
            device_id_type=MESH,
        )

    def j_start(j, c, value):
        wide = mul(perm[c], both(value))
        j_send[j, c] = wide[:, :lanes] + wide[:, lanes:]
        j_copy(j, c).start()

    def j_finish(j, c, value):
        j_copy(j, c).wait_recv()
        return mask[0, c].astype(F32) * (value - j_recv[j, c])

    def at(c):
        return pl.ds(c * dofs, dofs)

    def apply(high, low, c):
        return mul3(high[at(c), :], low[at(c), :], vec[...])

    def split_stage(high, low):
        def body(k, carry):
            part = pl.ds(pl.multiple_of(k * 128, 128), 128)
            h, l = split(stage[part, :])
            high[part, :] = h
            low[part, :] = l
            return carry

        lax.fori_loop(0, stage.shape[0] // 128, body, 0)

    def exchange(source, target, ssem, rsem):
        def copy(it, a, b, t, landing):
            return pltpu.make_async_remote_copy(
                src_ref=source(it, a, t), dst_ref=target.at[it, landing],
                send_sem=ssem.at[it, t], recv_sem=rsem.at[it, landing],
                device_id=(a, b), device_id_type=MESH,
            )

        return (
            lambda it: visit(lambda a, b, t: copy(it, a, b, t, me).start()),
            lambda it: visit(lambda a, b, t: copy(it, a, b, t, t).wait_recv()),
            lambda it: visit(lambda a, b, t: copy(it, a, b, t, me).wait_send()),
        )

    x_start, x_wait, x_drain = exchange(
        lambda it, a, t: packed.at[it, a], x_recv, x_ssem, x_rsem
    )
    z_start, z_wait, z_drain = exchange(lambda it, a, t: y_send.at[it, t], z_recv, z_ssem, z_rsem)
    d_start, d_wait, d_drain = exchange(lambda it, a, t: d_send.at[it], d_recv, d_ssem, d_rsem)

    lane = lax.broadcasted_iota(jnp.int32, (group_rows, lanes), 1) // own

    def coarse_send(it, rz_part):
        corner = mul3(cpl_hi[...], cpl_lo[...], vec[...])
        rz_sum = jnp.sum(rz_part, axis=0, keepdims=True)
        row = lax.broadcasted_iota(jnp.int32, (group_rows, lanes), 0)
        rz_rows = jnp.zeros((group_rows, lanes), F32)
        for k in range(n_sub):
            turn = (own * (groups - k)) % lanes
            moved = pltpu.roll(jnp.broadcast_to(rz_sum, (8, lanes)), turn, 1)[0:1, :]
            rz_rows = jnp.where((row == k) & (lane == groups), moved, rz_rows)
        for a in range(n_sub):
            total = rz_rows
            for g in range(groups):
                piece = corner[g * group_rows : (g + 1) * group_rows, :]
                turn = (own * (g - a)) % lanes
                moved = pltpu.roll(piece, turn, 1) if turn else piece
                total = jnp.where(lane == g, moved, total)
            packed[it, a] = total
        x_start(it)
        x_recv[it, me] = packed[it, my_sub]

    def coarse_solve(it):
        x_wait(it)
        whole = x_recv[it]
        rz_rows = jnp.sum(whole, axis=0)
        rz = jnp.zeros((group_rows, lanes), F32)
        for k in range(n_sub):
            turn = (own * (k - groups)) % lanes
            moved = pltpu.roll(rz_rows, turn, 1)
            rz = jnp.where(lane == k, moved[k : k + 1, :], rz)
        rz = rz[0:1, :]
        x = whole.reshape(n * group_rows, lanes)
        mine = lax.broadcasted_iota(jnp.int32, (n * group_rows, lanes), 1) // own
        total = jnp.zeros((rows, lanes), F32)
        size = n * group_rows
        for g in range(groups):
            wide = mul(pick[:, g * size : (g + 1) * size], both(jnp.where(mine == g, x, 0.0)))
            total = total + wide[:, :lanes] + wide[:, lanes:]
        gathered = total
        for k in range(1, n_sub):
            gathered = gathered + pltpu.roll(total, own * k, 1)
        pair = both(gathered)
        result = jnp.zeros((size, lanes), F32)
        for g in range(groups):
            part = slice(g * size, (g + 1) * size)
            result = jnp.where(mine == g, mul3(m_hi[part, :], m_lo[part, :], pair), result)
        y_send[it] = result.reshape(n, group_rows, lanes)
        z_start(it)
        z_recv[it, me] = y_send[it, me]
        return rz

    def coarse_back(it):
        z_wait(it)
        sums = [jnp.sum(z_recv[it, a * n_blk : (a + 1) * n_blk], axis=0) for a in range(n_sub)]
        pieces = []
        for g in range(groups):
            total = jnp.zeros((group_rows, lanes), F32)
            for a in range(n_sub):
                turn = (own * (a - g)) % lanes
                moved = pltpu.roll(sums[a], turn, 1) if turn else sums[a]
                total = jnp.where(lane == a, moved, total)
            pieces.append(total)
        return both(jnp.concatenate(pieces, axis=0))

    def dot_send(it, part):
        total = jnp.sum(part, axis=0, keepdims=True)
        d_send[it] = total
        d_start(it)
        d_recv[it, me] = total

    def dot_finish(it):
        d_wait(it)
        return jnp.sum(d_recv[it], axis=0)

    def absorb(high, low, index, c, value, target):
        pair = both(value)
        for k in ORDER:
            part = mul3(high[at(k), at(c)], low[at(k), at(c)], pair)
            target[k] = part if index == 0 else target[k] + part
            yield k

    for c in ORDER:
        j_start(0, c, face[0, c])
    load_dir.wait()
    split_stage(dir_hi, dir_lo)
    load_dual = pltpu.make_async_copy(dual.at[0], stage, local_sem.at[2])
    load_dual.start()
    cpl_hi[...], cpl_lo[...] = split(coupling[0])
    cplt_hi[...], cplt_lo[...] = split(coupling[0].T)
    for index, c in enumerate(ARRIVAL):
        r = j_finish(0, c, face[0, c])
        res[c] = r
        for k in absorb(dir_hi, dir_lo, index, c, r, y):
            if index == COLOURS - 1:
                j_start(1, k, y[k])
    load_dual.wait()
    split_stage(dual_hi, dual_lo)
    contract_last = (((1,), (1,)), ((), ()))
    for k in range(rows // chunk):
        if k:
            load_coarse[k].start()
        load_coarse[k].wait()
        coarse_hi[...], coarse_lo[...] = split(coarse_stage[...])
        batch = 512 if width <= 2048 else 128

        def select(i, carry):
            part = pl.ds(pl.multiple_of(i * batch, batch), batch)
            places = lax.broadcasted_iota(jnp.int32, (batch, width), 1)
            chosen = jnp.where(places == map_cols[part, 0:1], 1.0, 0.0).astype(BF16)
            for source, target in ((coarse_hi, m_hi), (coarse_lo, m_lo)):
                target[part, k * chunk : (k + 1) * chunk] = lax.dot_general(
                    chosen, source[...], contract_last, preferred_element_type=F32
                ).astype(BF16)
            return carry

        lax.fori_loop(0, m_hi.shape[0] // batch, select, 0)
    rz_part = jnp.zeros((8, lanes), F32)
    for c in ARRIVAL:
        p = j_finish(1, c, y[c])
        direc[c] = p
        vec[at(c), :] = both(p)
        rz_part = rz_part + fold(res[c] * p)

    alpha = None
    for it in range(ITERS):
        coarse_send(it, rz_part)
        for c in range(COLOURS):
            y[c] = apply(dual_hi, dual_lo, c)
        if it == 0:
            for g in range(groups):
                size = n * group_rows
                places = lax.broadcasted_iota(jnp.int32, (rows, size), 0) + my_blk * rows
                pick[:, g * size : (g + 1) * size] = jnp.where(
                    places == map_rows[g : g + 1, :], 1.0, 0.0
                ).astype(BF16)
        rz_new = coarse_solve(it)
        corners = coarse_back(it)
        for c in ORDER:
            y[c] = y[c] + mul3(cplt_hi[at(c), :], cplt_lo[at(c), :], corners)
            j_start(2 + 2 * it, c, y[c])
        part = jnp.zeros((8, lanes), F32)
        if it == 0:
            rz = rz_new
            for index, c in enumerate(ARRIVAL):
                i = j_finish(2, c, y[c])
                image[c] = i
                part = part + fold(direc[c] * i)
                for k in absorb(dir_hi, dir_lo, index, c, i, y_next):
                    if index == COLOURS - 1:
                        j_start(3, k, y_next[k])
            dot_send(0, part)
            alpha = rz / dot_finish(0)
            rz_part = jnp.zeros((8, lanes), F32)
            for c in ARRIVAL:
                r = res[c] - alpha * image[c]
                res[c] = r
                p = direc[c] - alpha * j_finish(3, c, y_next[c])
                step[c] = p
                vec[at(c), :] = both(p)
                rz_part = rz_part + fold(r * p)
        else:
            beta = rz_new / rz
            for c in ARRIVAL:
                i = j_finish(4, c, y[c]) + beta * image[c]
                image[c] = i
                p = step[c] + beta * direc[c]
                step[c] = p
                part = part + fold(p * i)
            dot_send(1, part)
            last = rz_new / dot_finish(1)
            scales[0:1, :] = alpha
            scales[1:2, :] = last

    for j in range(5):
        for c in range(COLOURS):
            j_copy(j, c).wait_send()
    for it in range(ITERS):
        x_drain(it)
        z_drain(it)
        d_drain(it)


def solution(mesh):
    n_sub, n_blk = mesh.shape["sub"], mesh.shape["blk"]
    n = n_sub * n_blk

    def shards(face, mask, dof, dual, dirichlet, coupling, corner_map, coarse):
        colours, dofs, lanes = face.shape[1:]
        local = colours * dofs
        corners = corner_map.shape[1]
        group_rows = -(-corners // (8 * n_sub)) * 8
        groups = corners // group_rows
        rows, width = coarse.shape
        chunk = rows if rows <= 192 else 128
        size = n * group_rows
        map_rows = (
            corner_map.reshape(n, groups, group_rows).transpose(1, 0, 2).reshape(groups, size)
        )
        map_cols = jnp.broadcast_to(map_rows.reshape(groups * size, 1), (groups * size, 128))
        vmem = pl.BlockSpec(memory_space=pltpu.VMEM)
        smem = pl.BlockSpec(memory_space=pltpu.SMEM)
        hbm = pl.BlockSpec(memory_space=pl.ANY)
        vector = pltpu.VMEM((colours, dofs, lanes), F32)
        dma = pltpu.SemaphoreType.DMA
        direc, step, res, image, scales = pl.pallas_call(
            functools.partial(kernel, n_sub, n_blk, group_rows, groups),
            out_shape=[jax.ShapeDtypeStruct(face.shape[1:], F32)] * 4
            + [jax.ShapeDtypeStruct((2, lanes), F32)],
            in_specs=[vmem, smem, vmem, hbm, hbm, vmem, vmem, vmem, hbm],
            out_specs=[vmem] * 5,
            scratch_shapes=[
                pltpu.VMEM((local, local), F32),
                pltpu.VMEM((local, local), BF16),
                pltpu.VMEM((local, local), BF16),
                pltpu.VMEM((local, local), BF16),
                pltpu.VMEM((local, local), BF16),
                pltpu.VMEM((colours, dofs, dofs), BF16),
                pltpu.VMEM((chunk, width), F32),
                pltpu.VMEM((chunk, width), BF16),
                pltpu.VMEM((chunk, width), BF16),
                pltpu.VMEM((groups * size, rows), BF16),
                pltpu.VMEM((groups * size, rows), BF16),
                pltpu.VMEM((rows, groups * size), BF16),
                pltpu.VMEM((corners, local), BF16),
                pltpu.VMEM((corners, local), BF16),
                pltpu.VMEM((local, corners), BF16),
                pltpu.VMEM((local, corners), BF16),
                pltpu.VMEM((local, 2 * lanes), BF16),
                vector, vector,
                pltpu.VMEM((5, colours, dofs, lanes), F32),
                pltpu.VMEM((5, colours, dofs, lanes), F32),
                pltpu.VMEM((ITERS, n_sub, group_rows, lanes), F32),
                pltpu.VMEM((ITERS, n, group_rows, lanes), F32),
                pltpu.VMEM((ITERS, n, group_rows, lanes), F32),
                pltpu.VMEM((ITERS, n, group_rows, lanes), F32),
                pltpu.VMEM((ITERS, 1, lanes), F32),
                pltpu.VMEM((ITERS, n, 1, lanes), F32),
                dma((3,)),
                dma((5, colours)), dma((5, colours)),
                dma((ITERS, n)), dma((ITERS, n)),
                dma((ITERS, n)), dma((ITERS, n)),
                dma((ITERS, n)), dma((ITERS, n)),
            ],
            compiler_params=pltpu.CompilerParams(
                collective_id=0, has_side_effects=True, vmem_limit_bytes=62 << 20
            ),
            cost_estimate=pl.CostEstimate(
                flops=3 * 8 * local * local * lanes, bytes_accessed=8 * local * local,
                transcendentals=0,
            ),
        )(face, mask, dof.transpose(1, 0, 2), dual, dirichlet, coupling, map_rows, map_cols, coarse)
        alpha, last = scales[0], scales[1]
        return (alpha * direc + last * step)[None], (res - last * image)[None]

    split_first = P(("sub", "blk"), None, None, None)
    return jax.shard_map(
        shards,
        mesh=mesh,
        in_specs=(
            split_first,
            P(("sub", "blk"), None),
            P(("sub", "blk"), None, None),
            P(("sub", "blk"), None, None),
            P(("sub", "blk"), None, None),
            P(("sub", "blk"), None, None),
            P(),
            P("blk", None),
        ),
        out_specs=(split_first, split_first),
        check_vma=False,
    )
```
